32 devices in a mesh: lat: 8 (over y, x, core), lon: 4 (over z).
Axes of the slice: x: 2, y: 2, z: 4, core: 2. Of those that a mesh axis runs over, the one named last changes fastest.
Arguments:
- fields: bfloat16 [32, 512, 192], P('lat', 'lon'), may hold values from -6 to 6
- kernel_first: bfloat16 [9, 192, 192], replicated, may hold values from -0.15625 to 0.15625
- kernel_second: bfloat16 [9, 192, 192], replicated, may hold values from -0.15625 to 0.15625
- kernel_third: bfloat16 [9, 192, 192], replicated, may hold values from -0.15625 to 0.15625
- cotangent: bfloat16 [32, 512, 192], P('lat', 'lon'), may hold values from -6 to 6
Outputs:
- output: float32 [32, 512, 192], P('lat', 'lon')
- field_grad: float32 [32, 512, 192], P('lat', 'lon')
- grad_first: float32 [9, 192, 192], P(None, None, 'lat')
- grad_second: float32 [9, 192, 192], P(None, None, 'lat')
- grad_third: float32 [9, 192, 192], P(None, None, 'lat')
The draws below stay inside these ranges and needn't reach their ends.
All inputs are finite; a program needn't handle non-finite values.
Results may differ from the reference program's by a relative error of at most 0.0049.
Values may be sent and summed in bfloat16 or wider, within the bound.
A program may use at most 64 MiB of HBM per device.

```python
import jax
import jax.numpy as jnp

C = 192
NLAT = 32
NLON = 512


def raised(entries, rng, source, target, parts, factor):
    def block_of(dim):
        return (jnp.arange(entries.shape[dim]) // (entries.shape[dim] // parts)).reshape((-1,) + (1,) * (entries.ndim - 1 - dim))

    first = jax.random.permutation(rng, parts)[block_of(target)]
    other_side = (block_of(target) + parts // 2) % parts
    return jnp.where((block_of(source) == first) | (block_of(source) == other_side), factor * entries, entries)


def level_of(key, dims, cuts, least, top_value):
    loudness, own = 1.0, jax.random.fold_in(key, 6)
    for dim, shards_of in cuts:
        draws = jnp.exp(jax.random.uniform(jax.random.fold_in(own, dim), (shards_of,), jnp.float32, least / len(cuts), top_value / len(cuts)))
        loudness = loudness * jnp.repeat(draws, dims[dim] // shards_of).reshape([-1 if axis == dim else 1 for axis in range(len(dims))])
    return loudness


def noise(key, dims, deviation, reach, split=(), dtype=jnp.bfloat16):
    result = jax.random.normal(key, dims, jnp.float32) * deviation
    if len(split) > 0:
        result = level_of(key, dims, split, -0.22, 0.18) * result
    return jnp.clip(result, min=-reach, max=reach).astype(dtype)


def bell_draw_with(stream_key, dims, scale, bound, shards, heavy, dtype=jnp.bfloat16):
    entries = scale * jax.random.normal(stream_key, dims, jnp.float32)
    if shards:
        entries = entries * level_of(stream_key, dims, shards, -0.22, 0.18)
    return jnp.clip(raised(entries, jax.random.fold_in(stream_key, 3), *heavy), -bound, bound).astype(dtype)


def setup_inputs(seed: int = 0) -> dict:
    keys = jax.random.split(jax.random.key(seed), 6)
    fields = noise(keys[0], (NLAT, NLON, C), 1.0, 6.0, ((0, 8), (1, 4)))
    kernel_first = noise(keys[1], (9, C, C), (9 * C) ** -0.5, 0.15625)
    kernel_second = noise(keys[2], (9, C, C), (9 * C) ** -0.5, 0.15625)
    kernel_third = noise(keys[3], (9, C, C), (9 * C) ** -0.5, 0.15625)
    cotangent = bell_draw_with(keys[4], (NLAT, NLON, C), 1.0, 6.0, ((0, 8), (1, 4)), (0, 2, 8, 2.0))
    return dict(fields=fields, kernel_first=kernel_first, kernel_second=kernel_second, kernel_third=kernel_third, cotangent=cotangent)


def gelu(z):
    return 0.5 * z * (1.0 + jax.scipy.special.erf(z * 0.7071067811865476))

def gelu_slope(z):
    return 0.5 * (1.0 + jax.scipy.special.erf(z * 0.7071067811865476)) + z * jnp.exp(-0.5 * z * z) * 0.3989422804014327

def pad_grid(field):
    field = jnp.pad(field, ((1, 1), (0, 0), (0, 0)))
    return jnp.concatenate([field[:, -1:], field, field[:, :1]], axis=1)

def forward_conv(field, kernel):
    padded = pad_grid(field)
    total = jnp.zeros((NLAT * NLON, C), jnp.float32)
    for tap in range(9):
        shift_a, shift_b = divmod(tap, 3)
        piece = padded[shift_a:shift_a + NLAT, shift_b:shift_b + NLON].reshape(NLAT * NLON, C)
        total = total + jnp.dot(piece, kernel[tap], preferred_element_type=jnp.float32)
    return total.reshape(NLAT, NLON, C)

def adjoint_conv(field, kernel):
    padded = pad_grid(field)
    total = jnp.zeros((NLAT * NLON, C), jnp.float32)
    for tap in range(9):
        shift_a, shift_b = divmod(tap, 3)
        piece = padded[2 - shift_a:2 - shift_a + NLAT, 2 - shift_b:2 - shift_b + NLON].reshape(NLAT * NLON, C)
        total = total + jnp.dot(piece, kernel[tap].T, preferred_element_type=jnp.float32)
    return total.reshape(NLAT, NLON, C)

def kernel_grad(field, delta):
    padded = pad_grid(field)
    flat_delta = delta.reshape(NLAT * NLON, C)
    scale = 1.0 / float(NLAT * NLON) ** 0.5
    terms = []
    for tap in range(9):
        shift_a, shift_b = divmod(tap, 3)
        piece = padded[shift_a:shift_a + NLAT, shift_b:shift_b + NLON].reshape(NLAT * NLON, C)
        terms.append(jnp.dot(piece.T, flat_delta, preferred_element_type=jnp.float32) * scale)
    return jnp.stack(terms)

def reference(fields, kernel_first, kernel_second, kernel_third, cotangent):
    pre_first = forward_conv(fields, kernel_first)
    act_first = gelu(pre_first).astype(jnp.bfloat16)
    pre_second = forward_conv(act_first, kernel_second)
    act_second = gelu(pre_second).astype(jnp.bfloat16)
    output = forward_conv(act_second, kernel_third)
    grad_third = kernel_grad(act_second, cotangent)
    delta_second = (adjoint_conv(cotangent, kernel_third) * gelu_slope(pre_second)).astype(jnp.bfloat16)
    grad_second = kernel_grad(act_first, delta_second)
    delta_first = (adjoint_conv(delta_second, kernel_second) * gelu_slope(pre_first)).astype(jnp.bfloat16)
    grad_first = kernel_grad(fields, delta_first)
    field_grad = adjoint_conv(delta_first, kernel_first)
    return (output, field_grad, grad_first, grad_second, grad_third)
```

```python
import functools

import jax
import jax.numpy as jnp
from jax import lax
from jax.experimental import pallas as pl
from jax.experimental.pallas import tpu as pltpu
from jax.sharding import PartitionSpec as P

MESH = pl.DeviceIdType.MESH
F32 = jnp.float32
BF16 = jnp.bfloat16
HALO = 4
SIDE = 8
SENT = 16
DIRS = ((-1, 0), (1, 0), (0, 1), (0, -1), (-1, 1), (-1, -1), (1, 1), (1, -1))


def gelu_and_slope(z):
    cdf = 0.5 * (1.0 + lax.erf(z * 0.7071067811865476))
    return z * cdf, cdf + z * jnp.exp(-0.5 * z * z) * 0.3989422804014327


def kernel(
    nlat, nlon, scale,
    fields, w1, w2, w3, cot,
    out, fgrad, g1, g2, g3,
    big_f, big_c, small_f, small_c,
    flat, xf, xc, xa1, xa2, xd2, xd1, slope1, slope2, wt1, wt2, wt3, ut,
    p1, r1, p2, r2, p3, r3,
    hs, hr, s1, v1, s2, v2, s3, v3,
):
    rows, cols, chan = fields.shape
    pitch = cols + 2 * SIDE
    lat, lon = lax.axis_index("lat"), lax.axis_index("lon")
    core, chip = lax.rem(lat, 2), lax.div(lat, 2)
    nchip = nlat // 2
    logs = p3.shape[1] - 1
    per = chan // nlat

    def at(dlat, dlon):
        return (lax.rem(lat + dlat + nlat, nlat), lax.rem(lon + dlon + nlon, nlon))

    halo_peers = [at(*d) for d in DIRS]
    pair = (chip * 2 + (1 - core), lon)
    plane = [(lax.rem(chip + j, nchip) * 2 + core, lon) for j in range(1, nchip)]
    plane_back = [(lax.rem(chip + nchip - j, nchip) * 2 + core, lon) for j in range(1, nchip)]

    def z_peer(s):
        bit = lax.rem(lax.div(lon, 1 << s), 2)
        return (lat, lon + (1 - 2 * bit) * (1 << s))

    z_peers = [z_peer(s) for s in range(logs)]
    barrier = pltpu.get_barrier_semaphore()
    peers = halo_peers + [pair] + plane + z_peers
    for peer in peers:
        pl.semaphore_signal(barrier, inc=1, device_id=peer, device_id_type=MESH)
    pl.semaphore_wait(barrier, len(peers))

    halo = []
    for which, (src, big, small) in enumerate(((fields, big_f, small_f), (cot, big_c, small_c))):
        copies = []
        for d, (dy, dx) in enumerate(DIRS):
            slot = DIRS.index((-dy, -dx))
            if dx == 0:
                source, target = src, big.at[slot]
            else:
                start = cols - SENT if dx == 1 else 0
                source, target = src.at[:, pl.ds(start, SENT), :], small.at[slot - 2]
            copies.append(pltpu.make_async_remote_copy(
                source, target, hs.at[which, d], hr.at[which, slot],
                device_id=halo_peers[d], device_id_type=MESH))
        for c in copies:
            c.start()
        halo.append(copies)

    for w, wt in ((w3, wt3), (w2, wt2), (w1, wt1)):
        for tap in range(9):
            a, b = divmod(8 - tap, 3)
            wt[a, b * chan:(b + 1) * chan, :] = (
                w[tap // 3, (tap % 3) * chan:(tap % 3 + 1) * chan, :].T)

    north = lat > 0
    south = lat < nlat - 1
    total = flat.shape[0]

    def assemble(src, big, small, x):
        for e in range(rows + 2 * HALO):
            br, rr = divmod(e, rows)
            base = 8 + 16 + pitch * e
            if br == 1:
                mid = src[rr].astype(F32)
                east, west = small[0, rr].astype(F32), small[1, rr].astype(F32)
            else:
                ok = north if br == 0 else south
                side = 0 if br == 0 else 1
                mid = jnp.where(ok, big[side, rr].astype(F32), 0.0)
                east = jnp.where(ok, small[2 + 2 * side, rr].astype(F32), 0.0)
                west = jnp.where(ok, small[3 + 2 * side, rr].astype(F32), 0.0)
            flat[base:base + cols, :] = mid
            flat[base + cols:base + cols + SIDE, :] = east[:SIDE]
            flat[base - SIDE:base, :] = west[SENT - SIDE:]
        spread(x, 0, rows + 2 * HALO)

    def spread(x, first, count):
        size = 2 * pitch + 16

        def body(k, _):
            q = pl.multiple_of((first + 2 * k) * pitch, 16)
            window = flat[pl.ds(q, size + 16), :]
            parts = [window[7 + b:7 + b + size].astype(BF16) for b in range(3)]
            x[pl.ds(q, size), :] = jnp.concatenate(parts, axis=1)
            return 0

        lax.fori_loop(0, count // 2, body, 0)

    def conv(x, w, start, size):
        acc = None
        for a in range(3):
            piece = x[pl.ds(pl.multiple_of(start + (a - 1) * pitch, 16), size), :]
            part = jnp.dot(piece, w[a], preferred_element_type=F32)
            acc = part if acc is None else acc + part
        return acc

    def valid(e):
        i = lax.broadcasted_iota(jnp.int32, (2 * pitch + 16, 1), 0)
        row = (e - 1 - HALO + lat * rows + (i >= 8).astype(jnp.int32)
               + (i >= 8 + pitch).astype(jnp.int32) + (i >= 8 + 2 * pitch).astype(jnp.int32))
        return (row >= 0) & (row < nlat * rows)

    def layer(x, w, first, count, finish):
        size = 2 * pitch + 16

        def body(k, _):
            e = first + 2 * k
            q = pl.multiple_of(e * pitch, 16)
            z = finish(conv(x, w, q, size), q)
            flat[pl.ds(q + 8, size), :] = jnp.where(valid(e), z, 0.0)
            return 0

        lax.fori_loop(0, count // 2, body, 0)

    def forward_finish(slope):
        def finish(z, q):
            act, s = gelu_and_slope(z)
            slope[pl.ds(q, z.shape[0]), :] = s
            return act.astype(BF16).astype(F32)
        return finish

    def adjoint_finish(slope):
        return lambda z, q: z * slope[pl.ds(q, z.shape[0]), :]

    def transpose_own(load):
        for k in range(rows):
            ut[:, k * cols:(k + 1) * cols] = load(k).T.astype(BF16)

    def own_flat(k):
        base = 8 + 16 + pitch * (HALO + k)
        return flat[base:base + cols, :]

    def last(x, w, dst):
        for k in range(rows):
            dst[k] = conv(x, w, 16 + pitch * (HALO + k), cols)

    def grad(x, g):
        parts = []
        for a in range(3):
            rhs = jnp.concatenate(
                [x[16 + pitch * (HALO + k + a - 1):16 + pitch * (HALO + k + a - 1) + cols, :]
                 for k in range(rows)], axis=0)
            parts.append(jnp.dot(ut[...], rhs, preferred_element_type=F32) * scale)
        tail = p1.shape[3] - 3 * per
        for d in range(nlat):
            pieces = [p[d * per:(d + 1) * per] for p in parts]
            if tail:
                pieces.append(jnp.zeros((tail, 3 * chan), F32))
            p1[g, d % 2, d // 2] = jnp.concatenate(pieces, axis=0).astype(BF16)
        c = pltpu.make_async_remote_copy(
            p1.at[g, 1 - core], r1.at[g], s1.at[g], v1.at[g],
            device_id=pair, device_id_type=MESH)
        c.start()
        sent.append(c)
        return c

    def to_plane(g, c):
        c.wait_recv()
        for k in range(nchip):
            p2[g, k] = (p1[g, core, k].astype(F32) + r1[g, k].astype(F32)).astype(BF16)
        copies = []
        for j in range(1, nchip):
            c = pltpu.make_async_remote_copy(
                p2.at[g, lax.rem(chip + j, nchip)], r2.at[g, j - 1], s2.at[g, j - 1],
                v2.at[g, j - 1], device_id=plane[j - 1], device_id_type=MESH)
            c.start()
            copies.append(c)
        sent.extend(copies)
        return copies

    def send_z(g, s):
        c = pltpu.make_async_remote_copy(
            p3.at[g, s], r3.at[g, s], s3.at[g, s], v3.at[g, s],
            device_id=z_peers[s], device_id_type=MESH)
        c.start()
        sent.append(c)
        return c

    def to_z(g, copies):
        acc = p2[g, chip].astype(F32)
        for j, c in enumerate(copies):
            c.wait_recv()
            acc = acc + r2[g, j].astype(F32)
        p3[g, 0] = acc.astype(BF16)
        return send_z(g, 0)

    def next_z(g, s, c):
        c.wait_recv()
        p3[g, s + 1] = (p3[g, s].astype(F32) + r3[g, s].astype(F32)).astype(BF16)
        return send_z(g, s + 1)

    def finish_z(g, c, dst):
        s = logs - 1
        c.wait_recv()
        dst[...] = p3[g, s].astype(F32) + r3[g, s].astype(F32)

    sent = []
    flat[0:16, :] = jnp.zeros((16, chan), F32)
    flat[total - 32:, :] = jnp.zeros((32, chan), F32)
    for c in halo[0]:
        c.wait_recv()
    assemble(fields, big_f, small_f, xf)
    layer(xf, w1, 1, 10, forward_finish(slope1))
    spread(xa1, 1, 10)
    layer(xa1, w2, 2, 8, forward_finish(slope2))
    spread(xa2, 2, 8)
    transpose_own(lambda k: cot[k].astype(F32))
    c3 = grad(xa2, 2)
    for c in halo[1]:
        c.wait_recv()
    assemble(cot, big_c, small_c, xc)
    layer(xc, wt3, 2, 8, adjoint_finish(slope2))
    transpose_own(own_flat)
    spread(xd2, 2, 8)
    c3 = to_plane(2, c3)
    c2 = grad(xa1, 1)
    layer(xd2, wt2, 3, 6, adjoint_finish(slope1))
    transpose_own(own_flat)
    spread(xd1, 3, 6)
    c1 = grad(xf, 0)
    c2 = to_plane(1, c2)
    c3 = to_z(2, c3)
    c1 = to_plane(0, c1)
    last(xa2, w3, out)
    cs = {2: c3}
    cs[1] = to_z(1, c2)
    last(xd1, wt1, fgrad)
    for s in range(logs - 1):
        cs[2] = next_z(2, s, cs[2])
    cs[0] = to_z(0, c1)
    for s in range(logs - 1):
        for g in (1, 0):
            cs[g] = next_z(g, s, cs[g])
    for g, dst in ((2, g3), (1, g2), (0, g1)):
        finish_z(g, cs[g], dst)
    for c in halo[0] + halo[1] + sent:
        c.wait_send()


def on_device(nlat, nlon, fields, kernel_first, kernel_second, kernel_third, cotangent):
    rows, cols, chan = fields.shape
    scale = 1.0 / float(rows * nlat * cols * nlon) ** 0.5
    per = chan // nlat
    nchip = nlat // 2
    logs = nlon.bit_length() - 1
    pitch = cols + 2 * SIDE
    length = pitch * (rows + 2 * HALO) + 32
    gr = -(-3 * per // 16) * 16
    wide = 3 * chan
    kernels = [k.reshape(3, wide, chan) for k in (kernel_first, kernel_second, kernel_third)]
    vm = pl.BlockSpec(memory_space=pltpu.VMEM)
    dma = pltpu.SemaphoreType.DMA
    x_shape = pltpu.VMEM((length, wide), BF16)
    flat_shape = pltpu.VMEM((length, chan), F32)
    wt_shape = pltpu.VMEM((3, wide, chan), BF16)
    outs = pl.pallas_call(
        functools.partial(kernel, nlat, nlon, scale),
        out_shape=[jax.ShapeDtypeStruct((rows, cols, chan), F32)] * 2
        + [jax.ShapeDtypeStruct((gr, wide), F32)] * 3,
        in_specs=[vm] * 5,
        out_specs=[vm] * 5,
        scratch_shapes=[
            pltpu.VMEM((2, rows, cols, chan), BF16),
            pltpu.VMEM((2, rows, cols, chan), BF16),
            pltpu.VMEM((6, rows, SENT, chan), BF16),
            pltpu.VMEM((6, rows, SENT, chan), BF16),
            pltpu.VMEM((length + 16, chan), F32),
            x_shape, x_shape, x_shape, x_shape, x_shape, x_shape,
            flat_shape, flat_shape,
            wt_shape, wt_shape, wt_shape,
            pltpu.VMEM((chan, rows * cols), BF16),
            pltpu.VMEM((3, 2, nchip, gr, wide), BF16),
            pltpu.VMEM((3, nchip, gr, wide), BF16),
            pltpu.VMEM((3, nchip, gr, wide), BF16),
            pltpu.VMEM((3, nchip - 1, gr, wide), BF16),
            pltpu.VMEM((3, logs + 1, gr, wide), BF16),
            pltpu.VMEM((3, logs, gr, wide), BF16),
            dma((2, 8)), dma((2, 8)),
            dma((3,)), dma((3,)),
            dma((3, nchip - 1)), dma((3, nchip - 1)),
            dma((3, logs)), dma((3, logs)),
        ],
        compiler_params=pltpu.CompilerParams(
            collective_id=0, has_side_effects=True, vmem_limit_bytes=60 * 1024 * 1024),
        name="block_backward",
    )(fields, *kernels, cotangent)
    grads = [
        g[:3 * per].reshape(3, per, 3, chan).transpose(0, 2, 3, 1).reshape(9, chan, per)
        for g in outs[2:]
    ]
    return (outs[0], outs[1], *grads)


def solution(mesh):
    in_specs = (P("lat", "lon", None), P(), P(), P(), P("lat", "lon", None))
    out_specs = (
        P("lat", "lon", None),
        P("lat", "lon", None),
        P(None, None, "lat"),
        P(None, None, "lat"),
        P(None, None, "lat"),
    )
    body = functools.partial(on_device, mesh.shape["lat"], mesh.shape["lon"])
    return jax.shard_map(
        body, mesh=mesh, in_specs=in_specs, out_specs=out_specs, check_vma=False
    )
```

```python
import functools

import jax
import jax.numpy as jnp
from jax import lax
from jax.experimental import pallas as pl
from jax.experimental.pallas import tpu as pltpu
from jax.sharding import PartitionSpec as P

MESH = pl.DeviceIdType.MESH
F32 = jnp.float32
BF16 = jnp.bfloat16
HALO = 4
SIDE = 8
SENT = 16
DIRS = ((-1, 0), (1, 0), (0, 1), (0, -1), (-1, 1), (-1, -1), (1, 1), (1, -1))


def gelu_and_slope(z):
    cdf = 0.5 * (1.0 + lax.erf(z * 0.7071067811865476))
    return z * cdf, cdf + z * jnp.exp(-0.5 * z * z) * 0.3989422804014327


def kernel(
    nlat, nlon, scale,
    fields, w1, w2, w3, cot,
    out, fgrad, g1, g2, g3,
    own_f, own_c, big_f, big_c, small_f, small_c,
    flat, acts, xf, xc, xa1, xa2, xd2, xd1, slope1, slope2, wt1, wt2, wt3, ut,
    p1, r1, p2, r2, p3, r3,
    hs, hr, s1, v1, s2, v2, s3, v3,
):
    rows, chan, cols = fields.shape
    pitch = cols + 2 * SIDE
    lat, lon = lax.axis_index("lat"), lax.axis_index("lon")
    core, chip = lax.rem(lat, 2), lax.div(lat, 2)
    nchip = nlat // 2
    logs = p3.shape[1] - 1
    per = chan // nlat

    def at(dlat, dlon):
        return (lax.rem(lat + dlat + nlat, nlat), lax.rem(lon + dlon + nlon, nlon))

    halo_peers = [at(*d) for d in DIRS]
    pair = (chip * 2 + (1 - core), lon)
    plane = [(lax.rem(chip + j, nchip) * 2 + core, lon) for j in range(1, nchip)]
    plane_back = [(lax.rem(chip + nchip - j, nchip) * 2 + core, lon) for j in range(1, nchip)]

    def z_peer(s):
        bit = lax.rem(lax.div(lon, 1 << s), 2)
        return (lat, lon + (1 - 2 * bit) * (1 << s))

    z_peers = [z_peer(s) for s in range(logs)]
    barrier = pltpu.get_barrier_semaphore()
    peers = halo_peers + [pair] + plane + z_peers
    for peer in peers:
        pl.semaphore_signal(barrier, inc=1, device_id=peer, device_id_type=MESH)
    north = lat > 0
    south = lat < nlat - 1

    def guarded(dy, action):
        if dy == 0:
            action()
        else:
            pl.when(north if dy < 0 else south)(action)

    for big, small, side, ok in (
        (big_f, small_f, 0, north), (big_f, small_f, 1, south),
        (big_c, small_c, 0, north), (big_c, small_c, 1, south),
    ):
        def clear(big=big, small=small, side=side):
            big[side] = jnp.zeros(big.shape[1:], BF16)
            for j in (2 + 2 * side, 3 + 2 * side):
                small[j] = jnp.zeros(small.shape[1:], BF16)

        pl.when(jnp.logical_not(ok))(clear)
    for k in range(rows):
        own_f[k] = fields[k].T
        own_c[k] = cot[k].T
    pl.semaphore_wait(barrier, len(peers))

    halo = []
    for which, (src, own, big, small) in enumerate(
        ((fields, own_f, big_f, small_f), (cot, own_c, big_c, small_c))
    ):
        deep = HALO - which
        copies = []
        for d, (dy, dx) in enumerate(DIRS):
            slot = DIRS.index((-dy, -dx))
            if dx == 0:
                part = pl.ds(0, deep) if dy < 0 else pl.ds(rows - deep, deep)
                source, target = src.at[part], big.at[slot, part]
            else:
                start = cols - SENT if dx == 1 else 0
                source, target = own.at[:, pl.ds(start, SENT), :], small.at[slot - 2]
            copies.append(pltpu.make_async_remote_copy(
                source, target, hs.at[which, d], hr.at[which, slot],
                device_id=halo_peers[d], device_id_type=MESH))
        for (dy, _), c in zip(DIRS, copies):
            guarded(dy, c.start)
        halo.append(copies)

    def arrived(which, d):
        dy, dx = DIRS[d]
        c = halo[which][DIRS.index((-dy, -dx))]
        guarded(dy, c.wait_recv)

    for w, wt in ((w3, wt3), (w2, wt2), (w1, wt1)):
        for tap in range(9):
            a, b = divmod(8 - tap, 3)
            wt[a, b * chan:(b + 1) * chan, :] = (
                w[tap // 3, (tap % 3) * chan:(tap % 3 + 1) * chan, :].T)

    total = flat.shape[0]

    def assemble(own, big, small, first, count):
        for e in range(first, first + count):
            br, rr = divmod(e, rows)
            base = 8 + 16 + pitch * e
            if br == 1:
                mid, j = own[rr], 0
            else:
                side = br // 2
                mid, j = big[side, rr].T, 2 + 2 * side
            flat[base:base + cols, :] = mid.astype(F32)
            flat[base + cols:base + cols + SIDE, :] = small[j, rr].astype(F32)[:SIDE]
            flat[base - SIDE:base, :] = small[j + 1, rr].astype(F32)[SENT - SIDE:]

    def spread(buf, x, first, count):
        size = 2 * pitch + 16

        def body(k, _):
            q = pl.multiple_of((first + 2 * k) * pitch, 16)
            window = buf[pl.ds(q, size + 16), :]
            parts = [window[7 + b:7 + b + size].astype(BF16) for b in range(3)]
            x[pl.ds(q, size), :] = jnp.concatenate(parts, axis=1)
            return 0

        lax.fori_loop(0, count // 2, body, 0)

    def conv(x, w, start, size):
        acc = None
        for a in range(3):
            piece = x[pl.ds(pl.multiple_of(start + (a - 1) * pitch, 16), size), :]
            part = jnp.dot(piece, w[a], preferred_element_type=F32)
            acc = part if acc is None else acc + part
        return acc

    def valid(e):
        i = lax.broadcasted_iota(jnp.int32, (2 * pitch + 16, 1), 0)
        row = (e - 1 - HALO + lat * rows + (i >= 8).astype(jnp.int32)
               + (i >= 8 + pitch).astype(jnp.int32) + (i >= 8 + 2 * pitch).astype(jnp.int32))
        return (row >= 0) & (row < nlat * rows)

    def layer(x, w, first, count, finish):
        size = 2 * pitch + 16

        def body(k, _):
            e = first + 2 * k
            q = pl.multiple_of(e * pitch, 16)
            z = finish(conv(x, w, q, size), q)
            acts[pl.ds(q + 8, size), :] = jnp.where(valid(e), z, 0.0)
            return 0

        lax.fori_loop(0, count // 2, body, 0)

    def forward_finish(slope):
        def finish(z, q):
            act, s = gelu_and_slope(z)
            slope[pl.ds(q, z.shape[0]), :] = s
            return act.astype(BF16).astype(F32)
        return finish

    def adjoint_finish(slope):
        return lambda z, q: z * slope[pl.ds(q, z.shape[0]), :]

    def transpose_own(load):
        for k in range(rows):
            ut[:, k * cols:(k + 1) * cols] = load(k).T.astype(BF16)

    def own_flat(k):
        base = 8 + 16 + pitch * (HALO + k)
        return acts[base:base + cols, :]

    def last(x, w, dst):
        for k in range(rows):
            dst[k] = conv(x, w, 16 + pitch * (HALO + k), cols).T

    def grad(x, g):
        parts = []
        for a in range(3):
            rhs = jnp.concatenate(
                [x[16 + pitch * (HALO + k + a - 1):16 + pitch * (HALO + k + a - 1) + cols, :]
                 for k in range(rows)], axis=0)
            parts.append(jnp.dot(ut[...], rhs, preferred_element_type=F32) * scale)
        tail = p1.shape[3] - 3 * per
        for d in range(nlat):
            pieces = [p[d * per:(d + 1) * per] for p in parts]
            if tail:
                pieces.append(jnp.zeros((tail, 3 * chan), F32))
            p1[g, d % 2, d // 2] = jnp.concatenate(pieces, axis=0).astype(BF16)
        c = pltpu.make_async_remote_copy(
            p1.at[g, 1 - core], r1.at[g], s1.at[g], v1.at[g],
            device_id=pair, device_id_type=MESH)
        c.start()
        sent.append(c)
        return c

    def to_plane(g, c):
        c.wait_recv()
        for k in range(nchip):
            p2[g, k] = (p1[g, core, k].astype(F32) + r1[g, k].astype(F32)).astype(BF16)
        copies = []
        for j in range(1, nchip):
            c = pltpu.make_async_remote_copy(
                p2.at[g, lax.rem(chip + j, nchip)], r2.at[g, j - 1], s2.at[g, j - 1],
                v2.at[g, j - 1], device_id=plane[j - 1], device_id_type=MESH)
            c.start()
            copies.append(c)
        sent.extend(copies)
        return copies

    def send_z(g, s):
        c = pltpu.make_async_remote_copy(
            p3.at[g, s], r3.at[g, s], s3.at[g, s], v3.at[g, s],
            device_id=z_peers[s], device_id_type=MESH)
        c.start()
        sent.append(c)
        return c

    def to_z(g, copies):
        acc = p2[g, chip].astype(F32)
        for j, c in enumerate(copies):
            c.wait_recv()
            acc = acc + r2[g, j].astype(F32)
        p3[g, 0] = acc.astype(BF16)
        return send_z(g, 0)

    def next_z(g, s, c):
        c.wait_recv()
        p3[g, s + 1] = (p3[g, s].astype(F32) + r3[g, s].astype(F32)).astype(BF16)
        return send_z(g, s + 1)

    def finish_z(g, c, dst):
        s = logs - 1
        c.wait_recv()
        total_sum = p3[g, s].astype(F32) + r3[g, s].astype(F32)
        for tap in range(9):
            a, b = divmod(tap, 3)
            dst[tap] = total_sum[a * per:(a + 1) * per, b * chan:(b + 1) * chan]

    sent = []
    for buf in (flat, acts):
        buf[0:16, :] = jnp.zeros((16, chan), F32)
        buf[total - 32:, :] = jnp.zeros((32, chan), F32)
    zeros = jnp.zeros((SIDE + pitch, chan), F32)
    flat[8 + pitch * HALO:16 + pitch * HALO, :] = zeros[:8]
    flat[8 + pitch * 2 * HALO:24 + pitch * 2 * HALO, :] = zeros[:16]
    acts[pitch:pitch + 8, :] = zeros[:8]
    acts[16 + 11 * pitch:24 + 11 * pitch, :] = zeros[:8]
    for d in (2, 3):
        arrived(0, d)
    assemble(own_f, big_f, small_f, rows, rows)
    spread(flat, xf, 4, 4)
    layer(xf, w1, 5, 2, forward_finish(slope1))
    for d in (0, 1, 4, 5, 6, 7):
        arrived(0, d)
    assemble(own_f, big_f, small_f, 0, rows)
    assemble(own_f, big_f, small_f, 2 * rows, rows)
    spread(flat, xf, 0, 4)
    spread(flat, xf, 8, 4)
    layer(xf, w1, 1, 4, forward_finish(slope1))
    layer(xf, w1, 7, 4, forward_finish(slope1))
    spread(acts, xa1, 1, 10)
    layer(xa1, w2, 2, 8, forward_finish(slope2))
    spread(acts, xa2, 2, 8)
    for k in range(rows):
        ut[:, k * cols:(k + 1) * cols] = cot[k]
    c3 = grad(xa2, 2)
    for d in range(8):
        arrived(1, d)
    big_c[0, 0] = jnp.zeros((chan, cols), BF16)
    big_c[1, rows - 1] = jnp.zeros((chan, cols), BF16)
    assemble(own_c, big_c, small_c, 0, 3 * rows)
    spread(flat, xc, 0, 12)
    layer(xc, wt3, 2, 8, adjoint_finish(slope2))
    transpose_own(own_flat)
    spread(acts, xd2, 2, 8)
    c3 = to_plane(2, c3)
    c2 = grad(xa1, 1)
    layer(xd2, wt2, 3, 6, adjoint_finish(slope1))
    transpose_own(own_flat)
    spread(acts, xd1, 3, 6)
    c1 = grad(xf, 0)
    c2 = to_plane(1, c2)
    c3 = to_z(2, c3)
    c1 = to_plane(0, c1)
    last(xa2, w3, out)
    cs = {2: c3}
    cs[1] = to_z(1, c2)
    last(xd1, wt1, fgrad)
    for s in range(logs - 1):
        cs[2] = next_z(2, s, cs[2])
    cs[0] = to_z(0, c1)
    for s in range(logs - 1):
        for g in (1, 0):
            cs[g] = next_z(g, s, cs[g])
    for g, dst in ((2, g3), (1, g2), (0, g1)):
        finish_z(g, cs[g], dst)
    for copies in halo:
        for (dy, _), c in zip(DIRS, copies):
            guarded(dy, c.wait_send)
    for c in sent:
        c.wait_send()


def on_device(nlat, nlon, fields, kernel_first, kernel_second, kernel_third, cotangent):
    rows, cols, chan = fields.shape
    scale = 1.0 / float(rows * nlat * cols * nlon) ** 0.5
    per = chan // nlat
    nchip = nlat // 2
    logs = nlon.bit_length() - 1
    pitch = cols + 2 * SIDE
    length = pitch * (rows + 2 * HALO) + 32
    gr = -(-3 * per // 16) * 16
    wide = 3 * chan
    kernels = [k.reshape(3, wide, chan) for k in (kernel_first, kernel_second, kernel_third)]
    vm = pl.BlockSpec(memory_space=pltpu.VMEM)
    dma = pltpu.SemaphoreType.DMA
    x_shape = pltpu.VMEM((length, wide), BF16)
    flat_shape = pltpu.VMEM((length, chan), F32)
    wt_shape = pltpu.VMEM((3, wide, chan), BF16)
    outs = pl.pallas_call(
        functools.partial(kernel, nlat, nlon, scale),
        out_shape=[jax.ShapeDtypeStruct((rows, chan, cols), F32)] * 2
        + [jax.ShapeDtypeStruct((9, per, chan), F32)] * 3,
        in_specs=[vm] * 5,
        out_specs=[vm] * 5,
        scratch_shapes=[
            pltpu.VMEM((rows, cols, chan), BF16),
            pltpu.VMEM((rows, cols, chan), BF16),
            pltpu.VMEM((2, rows, chan, cols), BF16),
            pltpu.VMEM((2, rows, chan, cols), BF16),
            pltpu.VMEM((6, rows, SENT, chan), BF16),
            pltpu.VMEM((6, rows, SENT, chan), BF16),
            pltpu.VMEM((length + 16, chan), F32),
            pltpu.VMEM((length + 16, chan), F32),
            x_shape, x_shape, x_shape, x_shape, x_shape, x_shape,
            flat_shape, flat_shape,
            wt_shape, wt_shape, wt_shape,
            pltpu.VMEM((chan, rows * cols), BF16),
            pltpu.VMEM((3, 2, nchip, gr, wide), BF16),
            pltpu.VMEM((3, nchip, gr, wide), BF16),
            pltpu.VMEM((3, nchip, gr, wide), BF16),
            pltpu.VMEM((3, nchip - 1, gr, wide), BF16),
            pltpu.VMEM((3, logs + 1, gr, wide), BF16),
            pltpu.VMEM((3, logs, gr, wide), BF16),
            dma((2, 8)), dma((2, 8)),
            dma((3,)), dma((3,)),
            dma((3, nchip - 1)), dma((3, nchip - 1)),
            dma((3, logs)), dma((3, logs)),
        ],
        compiler_params=pltpu.CompilerParams(
            collective_id=0, has_side_effects=True, vmem_limit_bytes=60 * 1024 * 1024),
        name="block_backward",
    )(fields.transpose(0, 2, 1), *kernels, cotangent.transpose(0, 2, 1))
    return tuple(x.transpose(0, 2, 1) for x in outs)


def solution(mesh):
    in_specs = (P("lat", "lon", None), P(), P(), P(), P("lat", "lon", None))
    out_specs = (
        P("lat", "lon", None),
        P("lat", "lon", None),
        P(None, None, "lat"),
        P(None, None, "lat"),
        P(None, None, "lat"),
    )
    body = functools.partial(on_device, mesh.shape["lat"], mesh.shape["lon"])
    return jax.shard_map(
        body, mesh=mesh, in_specs=in_specs, out_specs=out_specs, check_vma=False
    )
```

```python
import functools

import jax
import jax.numpy as jnp
from jax import lax
from jax.experimental import pallas as pl
from jax.experimental.pallas import tpu as pltpu
from jax.sharding import PartitionSpec as P

MESH = pl.DeviceIdType.MESH
F32 = jnp.float32
BF16 = jnp.bfloat16
HALO = 4
SIDE = 8
SENT = 16
DIRS = ((-1, 0), (1, 0), (0, 1), (0, -1), (-1, 1), (-1, -1), (1, 1), (1, -1))


def gelu_and_slope(z):
    cdf = 0.5 * (1.0 + lax.erf(z * 0.7071067811865476))
    return z * cdf, cdf + z * jnp.exp(-0.5 * z * z) * 0.3989422804014327


def kernel(
    nlat, nlon, scale,
    fields, w1, w2, w3, cot,
    out, fgrad, g1, g2, g3,
    own_f, own_c, big_f, big_c, small_f, small_c,
    flat, acts, xf, xc, xa1, xa2, xd2, xd1, slope1, slope2, wp1, wp2, wp3, wt1, wt2, wt3, ut,
    p1, r1, p2, r2, p3, r3,
    hs, hr, s1, v1, s2, v2, s3, v3,
):
    rows, chan, cols = fields.shape
    pitch = cols + 2 * SIDE
    lat, lon = lax.axis_index("lat"), lax.axis_index("lon")
    core, chip = lax.rem(lat, 2), lax.div(lat, 2)
    nchip = nlat // 2
    logs = p3.shape[1] - 1
    per = chan // nlat

    def at(dlat, dlon):
        return (lax.rem(lat + dlat + nlat, nlat), lax.rem(lon + dlon + nlon, nlon))

    halo_peers = [at(*d) for d in DIRS]
    pair = (chip * 2 + (1 - core), lon)
    plane = [(lax.rem(chip + j, nchip) * 2 + core, lon) for j in range(1, nchip)]
    plane_back = [(lax.rem(chip + nchip - j, nchip) * 2 + core, lon) for j in range(1, nchip)]

    def z_peer(s):
        bit = lax.rem(lax.div(lon, 1 << s), 2)
        return (lat, lon + (1 - 2 * bit) * (1 << s))

    z_peers = [z_peer(s) for s in range(logs)]
    barrier = pltpu.get_barrier_semaphore()
    peers = halo_peers + [pair] + plane + z_peers
    for peer in peers:
        pl.semaphore_signal(barrier, inc=1, device_id=peer, device_id_type=MESH)
    north = lat > 0
    south = lat < nlat - 1

    def guarded(dy, action):
        if dy == 0:
            action()
        else:
            pl.when(north if dy < 0 else south)(action)

    for big, small, side, ok in (
        (big_f, small_f, 0, north), (big_f, small_f, 1, south),
        (big_c, small_c, 0, north), (big_c, small_c, 1, south),
    ):
        def clear(big=big, small=small, side=side):
            big[side] = jnp.zeros(big.shape[1:], BF16)
            for j in (2 + 2 * side, 3 + 2 * side):
                small[j] = jnp.zeros(small.shape[1:], BF16)

        pl.when(jnp.logical_not(ok))(clear)
    for k in range(rows):
        own_f[k] = fields[k].T
        own_c[k] = cot[k].T
    pl.semaphore_wait(barrier, len(peers))

    halo = []
    for which, (src, own, big, small) in enumerate(
        ((fields, own_f, big_f, small_f), (cot, own_c, big_c, small_c))
    ):
        deep = HALO - which
        copies = []
        for d, (dy, dx) in enumerate(DIRS):
            slot = DIRS.index((-dy, -dx))
            if dx == 0:
                part = pl.ds(0, deep) if dy < 0 else pl.ds(rows - deep, deep)
                source, target = src.at[part], big.at[slot, part]
            else:
                start = cols - SENT if dx == 1 else 0
                source, target = own.at[:, pl.ds(start, SENT), :], small.at[slot - 2]
            copies.append(pltpu.make_async_remote_copy(
                source, target, hs.at[which, d], hr.at[which, slot],
                device_id=halo_peers[d], device_id_type=MESH))
        for (dy, _), c in zip(DIRS, copies):
            guarded(dy, c.start)
        halo.append(copies)

    def arrived(which, d):
        dy, dx = DIRS[d]
        c = halo[which][DIRS.index((-dy, -dx))]
        guarded(dy, c.wait_recv)

    padded = xf.shape[1]
    for w, wp, wt in ((w1, wp1, wt1), (w2, wp2, wt2), (w3, wp3, wt3)):
        for a in range(3):
            wp[a * padded:a * padded + 3 * chan, :] = w[a]
            for x in (wp, wt):
                if padded > 3 * chan:
                    x[a * padded + 3 * chan:(a + 1) * padded, :] = (
                        jnp.zeros((padded - 3 * chan, chan), BF16))
        for tap in range(9):
            a, b = divmod(8 - tap, 3)
            wt[a * padded + b * chan:a * padded + (b + 1) * chan, :] = (
                w[tap // 3, (tap % 3) * chan:(tap % 3 + 1) * chan, :].T)

    total = flat.shape[0]

    def assemble(own, big, small, first, count):
        for e in range(first, first + count):
            br, rr = divmod(e, rows)
            base = 8 + 16 + pitch * e
            if br == 1:
                mid, j = own[rr], 0
            else:
                side = br // 2
                mid, j = big[side, rr].T, 2 + 2 * side
            flat[base:base + cols, :] = mid.astype(F32)
            flat[base + cols:base + cols + SIDE, :] = small[j, rr].astype(F32)[:SIDE]
            flat[base - SIDE:base, :] = small[j + 1, rr].astype(F32)[SENT - SIDE:]

    def spread(buf, x, first, count):
        size = 2 * pitch + 16

        def body(k, _):
            q = pl.multiple_of((first + 2 * k) * pitch, 16)
            window = buf[pl.ds(q, size + 16), :]
            parts = [window[7 + b:7 + b + size].astype(BF16) for b in range(3)]
            if padded > 3 * chan:
                parts.append(jnp.zeros((size, padded - 3 * chan), BF16))
            x[pl.ds(q, size), :] = jnp.concatenate(parts, axis=1)
            return 0

        lax.fori_loop(0, count // 2, body, 0)

    def conv(x, w, start, size):
        pieces = [x[pl.ds(pl.multiple_of(start + (a - 1) * pitch, 16), size), :]
                  for a in range(3)]
        return jnp.dot(jnp.concatenate(pieces, axis=1), w[...], preferred_element_type=F32)

    def valid(e):
        i = lax.broadcasted_iota(jnp.int32, (2 * pitch + 16, 1), 0)
        row = (e - 1 - HALO + lat * rows + (i >= 8).astype(jnp.int32)
               + (i >= 8 + pitch).astype(jnp.int32) + (i >= 8 + 2 * pitch).astype(jnp.int32))
        return (row >= 0) & (row < nlat * rows)

    def layer(x, w, first, count, finish):
        size = 2 * pitch + 16

        def body(k, _):
            e = first + 2 * k
            q = pl.multiple_of(e * pitch, 16)
            z = finish(conv(x, w, q, size), q)
            acts[pl.ds(q + 8, size), :] = jnp.where(valid(e), z, 0.0)
            return 0

        lax.fori_loop(0, count // 2, body, 0)

    def forward_finish(slope):
        def finish(z, q):
            act, s = gelu_and_slope(z)
            slope[pl.ds(q, z.shape[0]), :] = s
            return act.astype(BF16).astype(F32)
        return finish

    def adjoint_finish(slope):
        return lambda z, q: z * slope[pl.ds(q, z.shape[0]), :]

    def transpose_own(load):
        for k in range(rows):
            ut[:, k * cols:(k + 1) * cols] = load(k).T.astype(BF16)

    def own_flat(k):
        base = 8 + 16 + pitch * (HALO + k)
        return acts[base:base + cols, :]

    def last(x, w, dst, first, count):
        for k in range(first, first + count):
            dst[k] = conv(x, w, 16 + pitch * (HALO + k), cols).T

    def grad(x, g):
        parts = []
        for a in range(3):
            rhs = jnp.concatenate(
                [x[16 + pitch * (HALO + k + a - 1):16 + pitch * (HALO + k + a - 1) + cols, :3 * chan]
                 for k in range(rows)], axis=0)
            parts.append(jnp.dot(ut[...], rhs, preferred_element_type=F32) * scale)
        tail = p1.shape[3] - 3 * per
        for d in range(nlat):
            pieces = [p[d * per:(d + 1) * per] for p in parts]
            if tail:
                pieces.append(jnp.zeros((tail, 3 * chan), F32))
            p1[g, d % 2, d // 2] = jnp.concatenate(pieces, axis=0).astype(BF16)
        c = pltpu.make_async_remote_copy(
            p1.at[g, 1 - core], r1.at[g], s1.at[g], v1.at[g],
            device_id=pair, device_id_type=MESH)
        c.start()
        sent.append(c)
        return c

    def to_plane(g, c):
        c.wait_recv()
        for k in range(nchip):
            p2[g, k] = (p1[g, core, k].astype(F32) + r1[g, k].astype(F32)).astype(BF16)
        copies = []
        for j in range(1, nchip):
            c = pltpu.make_async_remote_copy(
                p2.at[g, lax.rem(chip + j, nchip)], r2.at[g, j - 1], s2.at[g, j - 1],
                v2.at[g, j - 1], device_id=plane[j - 1], device_id_type=MESH)
            c.start()
            copies.append(c)
        sent.extend(copies)
        return copies

    gr = p3.shape[2]
    half = -(-gr // 32) * 16
    bit = lax.rem(lon, 2)

    def send_z(g, s):
        part = pl.ds(pl.multiple_of((1 - bit) * (gr - half), 16), half) if s == 0 else pl.ds(0, half)
        c = pltpu.make_async_remote_copy(
            p3.at[g, s, part], r3.at[g, s, pl.ds(0, half)], s3.at[g, s], v3.at[g, s],
            device_id=z_peers[s % logs], device_id_type=MESH)
        c.start()
        sent.append(c)
        return c

    def to_z(g, copies):
        acc = p1[g, core, chip].astype(F32) + r1[g, chip].astype(F32)
        for j, c in enumerate(copies):
            c.wait_recv()
            acc = acc + r2[g, j].astype(F32)
        p3[g, 0] = acc.astype(BF16)
        return send_z(g, 0)

    def next_z(g, s, c):
        c.wait_recv()
        part = pl.ds(pl.multiple_of(bit * (gr - half), 16), half) if s == 0 else pl.ds(0, half)
        p3[g, s + 1, 0:half] = (
            p3[g, s, part].astype(F32) + r3[g, s, 0:half].astype(F32)).astype(BF16)
        return send_z(g, s + 1)

    def finish_z(g, c, dst):
        c.wait_recv()
        mine = p3[g, logs, 0:half].astype(F32)
        other = r3[g, logs, 0:half].astype(F32)
        lower = jnp.where(bit == 0, mine, other)
        upper = jnp.where(bit == 0, other, mine)
        total_sum = jnp.concatenate([lower, upper[2 * half - gr:]], axis=0)
        for tap in range(9):
            a, b = divmod(tap, 3)
            dst[tap] = total_sum[a * per:(a + 1) * per, b * chan:(b + 1) * chan]

    sent = []
    for buf in (flat, acts):
        buf[0:16, :] = jnp.zeros((16, chan), F32)
        buf[total - 32:, :] = jnp.zeros((32, chan), F32)
    zeros = jnp.zeros((SIDE + pitch, chan), F32)
    flat[8 + pitch * HALO:16 + pitch * HALO, :] = zeros[:8]
    flat[8 + pitch * 2 * HALO:24 + pitch * 2 * HALO, :] = zeros[:16]
    acts[pitch:pitch + 8, :] = zeros[:8]
    acts[16 + 11 * pitch:24 + 11 * pitch, :] = zeros[:8]
    for d in (2, 3):
        arrived(0, d)
    assemble(own_f, big_f, small_f, rows, rows)
    spread(flat, xf, 4, 4)
    layer(xf, wp1, 5, 2, forward_finish(slope1))
    for d in (0, 1, 4, 5, 6, 7):
        arrived(0, d)
    assemble(own_f, big_f, small_f, 0, rows)
    assemble(own_f, big_f, small_f, 2 * rows, rows)
    spread(flat, xf, 0, 4)
    spread(flat, xf, 8, 4)
    layer(xf, wp1, 1, 4, forward_finish(slope1))
    layer(xf, wp1, 7, 4, forward_finish(slope1))
    spread(acts, xa1, 1, 10)
    layer(xa1, wp2, 2, 8, forward_finish(slope2))
    spread(acts, xa2, 3, 6)
    for k in range(rows):
        ut[:, k * cols:(k + 1) * cols] = cot[k]
    c3 = grad(xa2, 2)
    for d in range(8):
        arrived(1, d)
    assemble(own_c, big_c, small_c, 1, 3 * rows - 2)
    spread(flat, xc, 1, 10)
    c3 = to_plane(2, c3)
    layer(xc, wt3, 2, 8, adjoint_finish(slope2))
    transpose_own(own_flat)
    c2 = grad(xa1, 1)
    c3 = to_z(2, c3)
    spread(acts, xd2, 2, 8)
    layer(xd2, wt2, 3, 2, adjoint_finish(slope1))
    c2 = to_plane(1, c2)
    layer(xd2, wt2, 5, 4, adjoint_finish(slope1))
    transpose_own(own_flat)
    c1 = grad(xf, 0)
    cs = {2: c3}
    cs[2] = next_z(2, 0, cs[2])
    spread(acts, xd1, 3, 6)
    cs[1] = to_z(1, c2)
    c1 = to_plane(0, c1)
    last(xa2, wp3, out, 0, rows)
    last(xd1, wt1, fgrad, 0, rows // 2)
    cs[0] = to_z(0, c1)
    last(xd1, wt1, fgrad, rows // 2, rows - rows // 2)
    cs[1] = next_z(1, 0, cs[1])
    for s in range(1, logs):
        cs[2] = next_z(2, s, cs[2])
    cs[0] = next_z(0, 0, cs[0])
    for g in (1, 0):
        for s in range(1, logs):
            cs[g] = next_z(g, s, cs[g])
    for g, dst in ((2, g3), (1, g2), (0, g1)):
        finish_z(g, cs[g], dst)
    for copies in halo:
        for (dy, _), c in zip(DIRS, copies):
            guarded(dy, c.wait_send)
    for c in sent:
        c.wait_send()


def on_device(nlat, nlon, fields, kernel_first, kernel_second, kernel_third, cotangent):
    rows, cols, chan = fields.shape
    scale = 1.0 / float(rows * nlat * cols * nlon) ** 0.5
    per = chan // nlat
    nchip = nlat // 2
    logs = nlon.bit_length() - 1
    pitch = cols + 2 * SIDE
    length = pitch * (rows + 2 * HALO) + 32
    gr = -(-3 * per // 16) * 16
    wide = 3 * chan
    kernels = [k.reshape(3, wide, chan) for k in (kernel_first, kernel_second, kernel_third)]
    vm = pl.BlockSpec(memory_space=pltpu.VMEM)
    dma = pltpu.SemaphoreType.DMA
    padded = -(-wide // 128) * 128
    x_shape = pltpu.VMEM((length, padded), BF16)
    flat_shape = pltpu.VMEM((length, chan), F32)
    wt_shape = pltpu.VMEM((3 * padded, chan), BF16)
    outs = pl.pallas_call(
        functools.partial(kernel, nlat, nlon, scale),
        out_shape=[jax.ShapeDtypeStruct((rows, chan, cols), F32)] * 2
        + [jax.ShapeDtypeStruct((9, per, chan), F32)] * 3,
        in_specs=[vm] * 5,
        out_specs=[vm] * 5,
        scratch_shapes=[
            pltpu.VMEM((rows, cols, chan), BF16),
            pltpu.VMEM((rows, cols, chan), BF16),
            pltpu.VMEM((2, rows, chan, cols), BF16),
            pltpu.VMEM((2, rows, chan, cols), BF16),
            pltpu.VMEM((6, rows, SENT, chan), BF16),
            pltpu.VMEM((6, rows, SENT, chan), BF16),
            pltpu.VMEM((length + 16, chan), F32),
            pltpu.VMEM((length + 16, chan), F32),
            x_shape, x_shape, x_shape, x_shape, x_shape, x_shape,
            flat_shape, flat_shape,
            wt_shape, wt_shape, wt_shape,
            wt_shape, wt_shape, wt_shape,
            pltpu.VMEM((chan, rows * cols), BF16),
            pltpu.VMEM((3, 2, nchip, gr, wide), BF16),
            pltpu.VMEM((3, nchip, gr, wide), BF16),
            pltpu.VMEM((3, nchip, gr, wide), BF16),
            pltpu.VMEM((3, nchip - 1, gr, wide), BF16),
            pltpu.VMEM((3, logs + 1, gr, wide), BF16),
            pltpu.VMEM((3, logs + 1, gr, wide), BF16),
            dma((2, 8)), dma((2, 8)),
            dma((3,)), dma((3,)),
            dma((3, nchip - 1)), dma((3, nchip - 1)),
            dma((3, logs + 1)), dma((3, logs + 1)),
        ],
        compiler_params=pltpu.CompilerParams(
            collective_id=0, has_side_effects=True, vmem_limit_bytes=60 * 1024 * 1024),
        name="block_backward",
    )(fields.transpose(0, 2, 1), *kernels, cotangent.transpose(0, 2, 1))
    return tuple(x.transpose(0, 2, 1) for x in outs)


def solution(mesh):
    in_specs = (P("lat", "lon", None), P(), P(), P(), P("lat", "lon", None))
    out_specs = (
        P("lat", "lon", None),
        P("lat", "lon", None),
        P(None, None, "lat"),
        P(None, None, "lat"),
        P(None, None, "lat"),
    )
    body = functools.partial(on_device, mesh.shape["lat"], mesh.shape["lon"])
    return jax.shard_map(
        body, mesh=mesh, in_specs=in_specs, out_specs=out_specs, check_vma=False
    )
```
